128 devices in a mesh: vocab: 4 (over x_hi, core), dp: 32 (over x_lo, z, y).
Axes of the slice: x: 4 (x_hi: 2, x_lo: 2; x = x_hi * 2 + x_lo), y: 4, z: 4, core: 2. Of those that a mesh axis runs over, the one named last changes fastest.
Arguments:
- hidden: bfloat16 [4096, 7168], P('dp'), may hold values from -6 to 6
- gain: float32 [7168], replicated, may hold values from 0.25 to 1.75
- head_weight: bfloat16 [10240, 7168], P(('vocab', 'dp'))
- first_moment: float32 [10240, 7168], P(('vocab', 'dp')), may hold values from -0.12 to 0.12
- second_moment: float32 [10240, 7168], P(('vocab', 'dp')), may hold values from 0.0001 to 0.01
- targets: int32 [4096], P('dp'), may hold values from 0 to 10239
Outputs:
- grad_hidden: bfloat16 [4096, 7168], P('dp')
- grad_gain: float32 [7168], replicated
- new_weight: bfloat16 [10240, 7168], P(('vocab', 'dp'))
- new_first: float32 [10240, 7168], P(('vocab', 'dp'))
- new_second: float32 [10240, 7168], P(('vocab', 'dp'))
The draws below stay inside these ranges and needn't reach their ends.
All inputs are finite; a program needn't handle non-finite values.
Results may differ from the reference program's by a relative error of at most 0.007.
The reference program's roundings to bfloat16 on the way (of `normed` and `grad_logits`) count: a program that leaves them out, or rounds other values in their place, can miss the bound.
Values may be sent and summed in bfloat16 or wider, within the bound.
No kernel may reach another device: no remote copies, remote signals or barrier semaphores. Data moves between devices by JAX's collectives and lax.ppermute only.
A program may use at most 192 MiB of HBM per device.

```python
import math
import jax
import jax.numpy as jnp
import numpy as np
from jax import lax

D = 7168
STEP = 100
VOCAB = 10240
TOKENS = 4096


def draw_head_weight(key, part):
    key = jax.random.fold_in(key, 7)
    base = jax.random.normal(key, (VOCAB, D), jnp.float32) * (4.0 / jnp.sqrt(float(D)))
    return base.astype(jnp.bfloat16)


def set_ends(entries, own_key, least, largest):
    longest = entries.shape.index(max(entries.shape))
    spots = []
    for shift in (0, 1):
        where = [jax.random.randint(jax.random.fold_in(own_key, axis), (), 0, length) for axis, length in enumerate(entries.shape)]
        where[longest] = (where[longest] + shift) % entries.shape[longest]
        spots.append(tuple(where))
    return entries.at[spots[0]].set(least).at[spots[1]].set(largest)


def block_levels(rng, extent, pieces, least, top_value):
    def one(dim, blocks):
        draws = jax.random.uniform(jax.random.fold_in(jax.random.fold_in(rng, 6), dim), (blocks,), jnp.float32, least / len(pieces), top_value / len(pieces))
        return jnp.repeat(jnp.exp(draws), extent[dim] // blocks).reshape((-1,) + (1,) * (len(extent) - dim - 1))

    factor_of = one(*pieces[0])
    for cut in pieces[1:]:
        factor_of = factor_of * one(*cut)
    return factor_of


def rank_bounds(number_of, skew):
    loads = [(1 << 20) // math.isqrt(rank ** skew) + 1 for rank in range(1, number_of + 1)]
    spread = 1 + sum(loads) // (1 << 30)
    return np.cumsum(np.array([max(1, weight // spread) for weight in loads]))


def skewed_ids(own_key, shape, number_of, slope):
    table = rank_bounds(number_of, slope)
    pick = jax.random.randint(jax.random.fold_in(own_key, 1), shape, 0, int(table[number_of - 1]))
    standing = jnp.searchsorted(jnp.asarray(table, jnp.int32), pick, side="right")
    return jax.random.permutation(jax.random.fold_in(own_key, 2), number_of)[standing].astype(jnp.int32)


def bell_draw(own_key, extent, scale, reach, pieces=(), kind=jnp.bfloat16):
    drawn = scale * jax.random.normal(own_key, extent, jnp.float32)
    if pieces:
        drawn = drawn * block_levels(own_key, extent, pieces, -0.22, 0.18)
    return jnp.clip(drawn, -reach, reach).astype(kind)


def setup_inputs(seed: int = 0) -> dict:
    keys = jax.random.split(jax.random.key(seed), 7)
    hidden = bell_draw(keys[0], (TOKENS, D), 1.0, 6.0, ((0, 32),))
    gain = jnp.clip(1.0 + 0.15 * jax.random.normal(keys[1], (D,), jnp.float32), 0.25, 1.75)
    head_weight = draw_head_weight(jax.random.fold_in(keys[6], 71), 0)
    first_moment = bell_draw(keys[3], (VOCAB, D), 0.02, 0.12, ((0, 128),), jnp.float32)
    second_moment = jnp.clip(jnp.exp(math.log(0.01) - 4.6051702 * jax.random.uniform(keys[4], (VOCAB, D), jnp.float32) ** block_levels(keys[4], (VOCAB, D), ((0, 128),), -0.2, 0.2)), 0.0001, 0.01)
    targets = set_ends(skewed_ids(keys[5], (TOKENS,), VOCAB, 1), jax.random.fold_in(keys[5], 3), 0, VOCAB - 1).astype(jnp.int32)
    return {"hidden": hidden, "gain": gain, "head_weight": head_weight, "first_moment": first_moment, "second_moment": second_moment, "targets": targets}


def adam_step(weight, first, second, grads):
    new_first = 0.9 * first + 0.1 * grads
    new_second = 0.95 * second + 0.05 * grads * grads
    corr_one = 1.0 - 0.9 ** STEP
    corr_two = 1.0 - 0.95 ** STEP
    wfloat = weight.astype(jnp.float32)
    update = new_first / corr_one / (jnp.sqrt(new_second / corr_two) + 1e-08) + 0.1 * wfloat
    return ((wfloat - 0.001 * update).astype(jnp.bfloat16), new_first, new_second)

def reference(hidden, gain, head_weight, first_moment, second_moment, targets):
    hfloat = hidden.astype(jnp.float32)
    scale = lax.rsqrt(lax.optimization_barrier(jnp.mean(hfloat * hfloat, axis=-1, keepdims=True)) + 1e-06)
    normed = (hfloat * scale * gain).astype(jnp.bfloat16)
    logits = jnp.dot(normed, head_weight.T, preferred_element_type=jnp.float32)
    top = lax.optimization_barrier(jnp.max(logits, axis=-1, keepdims=True))
    expo = jnp.exp(logits - top)
    total = lax.optimization_barrier(jnp.sum(expo, axis=-1, keepdims=True))
    onehot = (targets[:, None] == jnp.arange(VOCAB, dtype=jnp.int32)[None, :]).astype(jnp.float32)
    grad_logits = (expo / total - onehot).astype(jnp.bfloat16)
    grad_normed = jnp.dot(grad_logits, head_weight, preferred_element_type=jnp.float32)
    scaled = grad_normed * gain
    dot_mean = lax.optimization_barrier(jnp.mean(scaled * hfloat, axis=-1, keepdims=True))
    grad_hidden = (scale * scaled - hfloat * scale ** 3 * dot_mean).astype(jnp.bfloat16)
    grad_gain = lax.optimization_barrier(jnp.sum(grad_normed * hfloat * scale, axis=0))
    grad_head = jnp.dot(grad_logits.T, normed, preferred_element_type=jnp.float32)
    new_weight, new_first, new_second = adam_step(head_weight, first_moment, second_moment, grad_head)
    return (grad_hidden, grad_gain, new_weight, new_first, new_second)
```

```python
import jax
import jax.numpy as jnp
from jax import lax
from jax.experimental import pallas as pl
from jax.experimental.pallas import tpu as pltpu
from jax.sharding import Mesh
from jax.sharding import PartitionSpec as P

STEP = 100
AXES = ("xh", "core", "xl", "z", "y")
SIZES = (2, 2, 2, 4, 4)
VMEM_LIMIT = 56 * 1024 * 1024
BLOCK = 1792
LANES = 128
half = jnp.bfloat16


def adam_step(weight, first, second, grads):
    new_first = 0.9 * first + 0.1 * grads
    new_second = 0.95 * second + 0.05 * grads * grads
    corr_one = 1.0 - 0.9**STEP
    corr_two = 1.0 - 0.95**STEP
    wfloat = weight.astype(jnp.float32)
    update = new_first / corr_one / (jnp.sqrt(new_second / corr_two) + 1e-08) + 0.1 * wfloat
    return ((wfloat - 0.001 * update).astype(jnp.bfloat16), new_first, new_second)


def place(x, core, z, y):
    index = 0
    for size, at in zip(SIZES, (x // 2, core, x % 2, z, y)):
        index = index * size + at
    return index


def move(array, step):
    pairs = []
    for x in range(4):
        for core in range(2):
            for z in range(4):
                for y in range(4):
                    x_to, core_to, z_to, y_to = step(x, core, z, y)
                    pairs.append((place(x, core, z, y), place(x_to % 4, core_to % 2, z_to % 4, y_to % 4)))
    return lax.ppermute(array, AXES, pairs)


def along_core(array):
    return move(array, lambda x, core, z, y: (x, core + 1, z, y))


def along_x(array, by):
    return move(array, lambda x, core, z, y: (x + by, core, z, y))


def flip_x(array):
    return move(array, lambda x, core, z, y: (x + 1 - 2 * core, core, z, y))


def along_y(array, by):
    return move(array, lambda x, core, z, y: (x, core, z, y + by * (1 - 2 * core)))


def along_z(array, by):
    return move(array, lambda x, core, z, y: (x, core, z + by * (1 - 2 * core), y))


def short(array):
    return array.astype(jnp.bfloat16)


def wide(array):
    return array.astype(jnp.float32)


def together(*arrays):
    return lax.optimization_barrier(arrays)


def merge(stats):
    top = jnp.max(stats[:, 0], axis=0)
    total = jnp.sum(stats[:, 1] * jnp.exp(stats[:, 0] - top), axis=0)
    return jnp.stack([top, total])


def strips(pieces):
    return [pl.BlockSpec((piece.shape[0], BLOCK), lambda i: (0, i)) for piece in pieces]


def whole(shape):
    return pl.BlockSpec(shape, lambda i: (0,) * len(shape))


def anywhere(arrays):
    return [pl.BlockSpec(memory_space=pl.ANY) for _ in arrays]


def params():
    return pltpu.CompilerParams(vmem_limit_bytes=VMEM_LIMIT)


def cost(rows, columns, depth):
    return pl.CostEstimate(
        flops=2 * rows * columns * depth, bytes_accessed=2 * depth * (rows + columns), transcendentals=0
    )


def by_strips(step, operands, outs, after=(), passed=()):
    width = operands[0][0].shape[1]
    block = 2 * BLOCK

    def kernel(*refs):
        taken = refs[: len(operands)]
        given = refs[len(operands) + len(after) + len(passed) :]
        for ref, value in zip(given, step(*[ref[...] for ref in taken])):
            ref[...] = value.astype(ref.dtype)

    def strip(rows, at=0):
        return pl.BlockSpec((rows, block), lambda i: (at, i))

    size = sum(rows for _, _, rows in operands) + sum(rows for rows, _ in outs)
    return pl.pallas_call(
        kernel,
        grid=(width // block,),
        in_specs=[strip(rows, start // rows) for _, start, rows in operands]
        + anywhere(after)
        + anywhere(passed),
        out_specs=[strip(rows) for rows, _ in outs] + anywhere(passed),
        out_shape=[jax.ShapeDtypeStruct((rows, width), dtype) for rows, dtype in outs]
        + [jax.ShapeDtypeStruct(array.shape, array.dtype) for array in passed],
        input_output_aliases={len(operands) + len(after) + i: len(outs) + i for i in range(len(passed))},
        compiler_params=params(),
        cost_estimate=pl.CostEstimate(flops=0, bytes_accessed=2 * size * width, transcendentals=0),
    )(*[array for array, _, _ in operands], *after, *passed)


def all_rows(*arrays):
    return [(array, 0, array.shape[0]) for array in arrays]


def norm_kernel(core_ref, hidden_ref, gain_ref, digits_ref, own_ref):
    width = hidden_ref.shape[1]
    hfloat = wide(hidden_ref[...])
    scale = lax.rsqrt(jnp.mean(hfloat * hfloat, axis=-1, keepdims=True) + 1e-06)
    own_ref[:, :width] = short(hfloat * scale * gain_ref[...])
    own_ref[:, width:] = digits_ref[...]


def normed_half(hidden, gain, digits, core):
    rows, width = hidden.shape
    block = rows // 4
    return pl.pallas_call(
        norm_kernel,
        grid_spec=pltpu.PrefetchScalarGridSpec(
            num_scalar_prefetch=1,
            grid=(2,),
            in_specs=[
                pl.BlockSpec((block, width), lambda i, core_ref: (core_ref[0] * 2 + i, 0)),
                pl.BlockSpec((1, width), lambda i, core_ref: (0, 0)),
                pl.BlockSpec((block, LANES), lambda i, core_ref: (core_ref[0] * 2 + i, 0)),
            ],
            out_specs=pl.BlockSpec((block, width + LANES), lambda i, core_ref: (i, 0)),
        ),
        out_shape=jax.ShapeDtypeStruct((rows // 2, width + LANES), half),
        compiler_params=params(),
        cost_estimate=pl.CostEstimate(flops=0, bytes_accessed=16 * rows * width, transcendentals=0),
    )(core.reshape(1), hidden, gain.reshape(1, width), digits)


def stack_of(refs):
    return jnp.concatenate([ref[...] for ref in refs], axis=0)


def logits_kernel(n_head, n_token, *refs):
    head = stack_of(refs[:n_head])
    tokens = stack_of(refs[n_head : n_head + n_token])
    digit_refs = refs[n_head + n_token : n_head + 2 * n_token]
    logits_ref, stats_ref = refs[-2:]
    product = lax.dot_general(head, tokens, (((1,), (1,)), ((), ())), preferred_element_type=jnp.float32)
    step = pl.program_id(0)

    @pl.when(step == 0)
    def _():
        logits_ref[...] = product

    @pl.when(step > 0)
    def _():
        logits_ref[...] += product

    @pl.when(step == pl.num_programs(0) - 1)
    def _():
        logits = logits_ref[...]
        top = jnp.max(logits, axis=0, keepdims=True)
        stats_ref[0:1, :] = top
        stats_ref[1:2, :] = jnp.sum(jnp.exp(logits - top), axis=0, keepdims=True)
        digits = wide(stack_of(digit_refs)).T
        stats_ref[2:3, :] = digits[0:1, :] * float(LANES) + digits[1:2, :]


def all_logits(head, tokens, after=()):
    rows, columns = (sum(piece.shape[0] for piece in pieces) for pieces in (head, tokens))
    width = head[0].shape[1]
    digits = [pl.BlockSpec((piece.shape[0], LANES), lambda i: (0, width // LANES)) for piece in tokens]
    return pl.pallas_call(
        lambda *refs: logits_kernel(len(head), len(tokens), *refs),
        grid=(width // BLOCK,),
        in_specs=strips(head) + strips(tokens) + digits + anywhere(after),
        out_specs=[whole((rows, columns)), whole((3, columns))],
        out_shape=[
            jax.ShapeDtypeStruct((rows, columns), jnp.float32),
            jax.ShapeDtypeStruct((3, columns), jnp.float32),
        ],
        compiler_params=params(),
        cost_estimate=cost(rows, columns, width),
    )(*head, *tokens, *tokens, *after)


def spread(product, outs, part):
    for k, ref in enumerate(outs):
        ref[...] = product[k * part : (k + 1) * part]


def token_grad_kernel(n_head, part, near_ref, flip_ref, stats_ref, wanted_ref, *refs):
    grads_ref = refs[n_head]
    outs, turned_ref = refs[n_head + 1 : -1], refs[-1]

    @pl.when(pl.program_id(0) == 0)
    def _():
        logits = jnp.concatenate([near_ref[...], flip_ref[...]], axis=1)
        rows = lax.broadcasted_iota(jnp.int32, logits.shape, 0)
        share = jnp.exp(logits - stats_ref[0:1, :]) / stats_ref[1:2, :]
        grads = share - jnp.where(rows == wanted_ref[...], 1.0, 0.0)
        grads_ref[...] = short(grads)
        turned_ref[...] = short(grads.T)

    product = jnp.dot(turned_ref[...], stack_of(refs[:n_head]), preferred_element_type=jnp.float32)
    spread(short(product), outs, part)


def token_grads(near, flip, stats, wanted, head):
    rows, columns = near.shape[0], near.shape[1] * 2
    width, part = head[0].shape[1], columns // 8
    return pl.pallas_call(
        lambda *refs: token_grad_kernel(len(head), part, *refs),
        grid=(width // BLOCK,),
        in_specs=[whole(near.shape), whole(flip.shape), whole((2, columns)), whole((1, columns))] + strips(head),
        out_specs=[whole((rows, columns))] + [pl.BlockSpec((part, BLOCK), lambda i: (0, i))] * 8,
        out_shape=[jax.ShapeDtypeStruct((rows, columns), half)] + [jax.ShapeDtypeStruct((part, width), half)] * 8,
        scratch_shapes=[pltpu.VMEM((columns, rows), half)],
        compiler_params=params(),
        cost_estimate=cost(rows, columns, width),
    )(near, flip, stats, wanted, *head)


def head_grad_kernel(n_head, n_token, grads_ref, *refs):
    near_ref, other_ref, gain_ref = refs[n_head + n_token :]
    tokens = stack_of(refs[n_head : n_head + n_token])
    product = jnp.dot(grads_ref[...], tokens, preferred_element_type=jnp.float32)
    rows = near_ref.shape[0]
    near_ref[...] = product[:rows]
    other_ref[...] = short(product[rows:])
    gain_ref[...] = jnp.sum(product * wide(stack_of(refs[:n_head])), axis=0, keepdims=True)


def head_grads(grads, head, tokens):
    rows, columns = grads.shape
    width = head[0].shape[1]
    return pl.pallas_call(
        lambda *refs: head_grad_kernel(len(head), len(tokens), *refs),
        grid=(width // BLOCK,),
        in_specs=[whole((rows, columns))] + strips(head) + strips(tokens),
        out_specs=[pl.BlockSpec((size, BLOCK), lambda i: (0, i)) for size in (rows // 2, rows // 2, 1)],
        out_shape=[
            jax.ShapeDtypeStruct((rows // 2, width), jnp.float32),
            jax.ShapeDtypeStruct((rows // 2, width), half),
            jax.ShapeDtypeStruct((1, width), jnp.float32),
        ],
        compiler_params=params(),
        cost_estimate=cost(rows, columns, width),
    )(grads, *head, *tokens)


def hidden_grad_kernel(core_ref, mine_ref, their_ref, hidden_ref, gain_ref, *refs):
    hfloat = wide(hidden_ref[...])
    scale = lax.rsqrt(jnp.mean(hfloat * hfloat, axis=-1, keepdims=True) + 1e-06)
    scaled = (wide(mine_ref[...]) + wide(their_ref[...])) * gain_ref[...]
    dot_mean = jnp.mean(scaled * hfloat, axis=-1, keepdims=True)
    refs[-1][...] = short(scale * scaled - hfloat * scale**3 * dot_mean)


def hidden_grads(mine, their, hidden, gain, core, after):
    rows, width = hidden.shape
    block = rows // 4
    return pl.pallas_call(
        hidden_grad_kernel,
        grid_spec=pltpu.PrefetchScalarGridSpec(
            num_scalar_prefetch=1,
            grid=(2,),
            in_specs=[
                pl.BlockSpec((block, width), lambda i, core_ref: (i, 0)),
                pl.BlockSpec((block, width), lambda i, core_ref: (i, 0)),
                pl.BlockSpec((block, width), lambda i, core_ref: (core_ref[0] * 2 + i, 0)),
                pl.BlockSpec((1, width), lambda i, core_ref: (0, 0)),
            ]
            + anywhere(after),
            out_specs=pl.BlockSpec((block, width), lambda i, core_ref: (i, 0)),
        ),
        out_shape=jax.ShapeDtypeStruct((rows // 2, width), half),
        compiler_params=params(),
        cost_estimate=pl.CostEstimate(flops=0, bytes_accessed=4 * rows * width, transcendentals=0),
    )(core.reshape(1), mine, their, hidden, gain.reshape(1, width), *after)


def local(hidden, gain, head_weight, first_moment, second_moment, targets):
    core = lax.axis_index("core")
    rows, width = hidden.shape
    held = head_weight.shape[0]
    part = rows // 2

    lane = lax.broadcasted_iota(jnp.int32, (rows, LANES), 1)
    wanted = targets[:, None]
    digits = jnp.where(lane == 0, wanted // LANES, jnp.where(lane == 1, wanted % LANES, 0)).astype(half)
    head_after, head_before = along_z(head_weight, -1), along_z(head_weight, 1)
    own = normed_half(hidden, gain, digits, core)
    own_after, own_before = along_y(own, -1), along_y(own, 1)
    flip_own = flip_x(own)
    own_after, own_before, flip_own = together(own_after, own_before, flip_own)
    own_far = along_y(own_after, -1)
    flip_after = flip_x(own_after)
    head_far = along_z(head_after, -1)
    other_own, other_after, other_before = (along_core(block) for block in (head_weight, head_after, head_before))
    own_far, flip_after = together(own_far, flip_after)
    flip_before = along_y(flip_own, 1)
    flip_far = flip_x(own_far)
    other_far = along_core(head_far)

    head = [head_weight, head_after, head_far, head_before, other_own, other_after, other_far, other_before]
    near_tokens = [own, own_after, own_far, own_before]
    flip_tokens = [flip_own, flip_after, flip_far, flip_before]
    near_logits, near_stats = all_logits(head, near_tokens)
    flip_logits, flip_stats = all_logits(head, flip_tokens, after=[near_stats])

    stats = jnp.stack([near_stats[:2], flip_stats[:2]], axis=1).reshape(2, 2, 4, part)
    stats = merge(jnp.stack([stats] + [jnp.roll(along_y(stats, by), -by, axis=2) for by in (1, 2, 3)]))
    stats = merge(jnp.stack([stats] + [jnp.roll(along_x(stats, by), by, axis=1) for by in (1, 2, 3)]))
    stats = stats.reshape(2, 8 * part)
    wanted = jnp.concatenate([near_stats[2:], flip_stats[2:]], axis=1).astype(jnp.int32)
    z, others = lax.axis_index("z"), lax.axis_index("xl") * 16 + lax.axis_index("y")
    spot = jnp.full_like(wanted, -1)
    for other in range(2):
        at_core = (core + other) % 2
        block = lax.axis_index("xh") * 2 + at_core
        for step in range(4):
            start = (block * 32 + others + (z + step * (1 - 2 * at_core)) % 4 * 4) * held
            inside = (wanted >= start) & (wanted < start + held)
            spot = jnp.where(inside, wanted - start + (other * 4 + step) * held, spot)

    grads, sum_own, sum_after, sum_far, sum_before, flip_own, flip_after, flip_far, flip_before = token_grads(
        near_logits, flip_logits, stats, spot, head
    )
    flip_far = flip_x(flip_far)
    flip_before = along_y(flip_before, -1)
    near_head, other_head, gain_sum = head_grads(grads, head, near_tokens + flip_tokens)

    sum_far, gain_sum, other_head, flip_after, sum_before = by_strips(
        lambda far, f_far, g_sum: (wide(far) + wide(f_far), g_sum),
        all_rows(sum_far, flip_far, gain_sum),
        [(part, half), (1, jnp.float32)],
        after=[flip_before],
        passed=[other_head, flip_after, sum_before],
    )
    sum_far = along_y(sum_far, 1)
    flip_after = flip_x(flip_after)
    other_head = along_core(other_head)
    sum_before = along_y(sum_before, -1)
    gain_sum = gain_sum + move(gain_sum, lambda x, core, z, y: (x, core, z ^ 1, y))
    gain_other = move(gain_sum, lambda x, core, z, y: (x, core, z + 2, y))
    head_far, head_before, gain_sum = by_strips(
        lambda mine, theirs, mine_too, theirs_too, g_sum, g_other: (
            mine + wide(theirs),
            mine_too + wide(theirs_too),
            g_sum + g_other,
        ),
        [(near_head, 2 * held, held), (other_head, 2 * held, held)]
        + [(near_head, 3 * held, held), (other_head, 3 * held, held)]
        + all_rows(gain_sum, gain_other),
        [(held, half), (held, half), (1, jnp.float32)],
    )

    sum_after, flip_own, head_far, head_before, gain_sum = by_strips(
        lambda after, f_after, far, own, before: (wide(after) + wide(f_after) + wide(far), wide(own) + wide(before)),
        all_rows(sum_after, flip_after, sum_far, flip_own, flip_before),
        [(part, half), (part, half)],
        after=[sum_before],
        passed=[head_far, head_before, gain_sum],
    )
    sum_after = along_y(sum_after, 1)
    flip_own = flip_x(flip_own)
    head_far, head_before = along_z(head_far, 1), along_z(head_before, -1)
    gain_sum = gain_sum + along_core(gain_sum)
    gain_other = move(gain_sum, lambda x, core, z, y: (x ^ 1, core, z, y))

    summed, gain_sum = by_strips(
        lambda a, b, c, d, mine, theirs: (wide(a) + wide(b) + (wide(c) + wide(d)), mine + theirs),
        all_rows(sum_own, flip_own, sum_after, sum_before, gain_sum, gain_other),
        [(part, half), (1, jnp.float32)],
    )
    (head_after,) = by_strips(
        lambda mine, theirs, far: (mine + wide(theirs) + wide(far),),
        [(near_head, held, held), (other_head, held, held), (head_far, 0, held)],
        [(held, half)],
        after=[summed],
    )
    head_after = along_z(head_after, 1)
    grad_hidden = hidden_grads(summed, along_x(summed, 2), hidden, gain, core, [head_after])
    other_half = along_core(grad_hidden)
    grad_hidden = jnp.where(
        core == 0,
        jnp.concatenate([grad_hidden, other_half]),
        jnp.concatenate([other_half, grad_hidden]),
    )

    gain_sum = gain_sum + move(gain_sum, lambda x, core, z, y: (x, core, z, y ^ 1))
    gain_sum = gain_sum + move(gain_sum, lambda x, core, z, y: (x, core, z, y + 2))
    grad_gain = gain_sum + along_x(gain_sum, 2)
    grad_gain = grad_gain.reshape(width) / gain

    grad_head = near_head[:held] + wide(other_head[:held]) + wide(head_after) + wide(head_before)
    new_weight, new_first, new_second = adam_step(head_weight, first_moment, second_moment, grad_head)
    return (grad_hidden, grad_gain, new_weight, new_first, new_second)


def solution(mesh):
    fine = Mesh(mesh.devices.reshape(SIZES), AXES)
    dp = ("xl", "z", "y")
    rows = P(AXES, None)
    return jax.shard_map(
        local,
        mesh=fine,
        in_specs=(P(dp, None), P(), rows, rows, rows, P(dp)),
        out_specs=(P(dp, None), P(), rows, rows, rows),
        check_vma=False,
    )
```

```python
import jax
import jax.numpy as jnp
from jax import lax
from jax.experimental import pallas as pl
from jax.experimental.pallas import tpu as pltpu
from jax.sharding import Mesh
from jax.sharding import PartitionSpec as P

STEP = 100
AXES = ("xh", "core", "xl", "z", "y")
SIZES = (2, 2, 2, 4, 4)
MIB = 1024 * 1024
BLOCK = 1792
LANES = 128
half = jnp.bfloat16


def adam_step(weight, first, second, grads):
    new_first = 0.9 * first + 0.1 * grads
    new_second = 0.95 * second + 0.05 * grads * grads
    corr_one = 1.0 - 0.9**STEP
    corr_two = 1.0 - 0.95**STEP
    wfloat = weight.astype(jnp.float32)
    update = new_first / corr_one / (jnp.sqrt(new_second / corr_two) + 1e-08) + 0.1 * wfloat
    return ((wfloat - 0.001 * update).astype(jnp.bfloat16), new_first, new_second)


def place(x, core, z, y):
    index = 0
    for size, at in zip(SIZES, (x // 2, core, x % 2, z, y)):
        index = index * size + at
    return index


def move(array, step):
    pairs = []
    for x in range(4):
        for core in range(2):
            for z in range(4):
                for y in range(4):
                    x_to, core_to, z_to, y_to = step(x, core, z, y)
                    pairs.append((place(x, core, z, y), place(x_to % 4, core_to % 2, z_to % 4, y_to % 4)))
    return lax.ppermute(array, AXES, pairs)


def along_core(array):
    return move(array, lambda x, core, z, y: (x, core + 1, z, y))


def along_x(array, by):
    return move(array, lambda x, core, z, y: (x + by, core, z, y))


def flip_x(array):
    return move(array, lambda x, core, z, y: (x + 1 - 2 * core, core, z, y))


def along_y(array, by):
    return move(array, lambda x, core, z, y: (x, core, z, y + by * (1 - 2 * core)))


def along_z(array, by):
    return move(array, lambda x, core, z, y: (x, core, z + by * (1 - 2 * core), y))


def short(array):
    return array.astype(jnp.bfloat16)


def wide(array):
    return array.astype(jnp.float32)


def together(*arrays):
    return lax.optimization_barrier(arrays)


def merge(stats):
    top = jnp.max(stats[:, 0], axis=0)
    total = jnp.sum(stats[:, 1] * jnp.exp(stats[:, 0] - top), axis=0)
    return jnp.stack([top, total])


def strips(pieces):
    return [pl.BlockSpec((piece.shape[0], BLOCK), lambda i: (0, i)) for piece in pieces]


def whole(shape):
    return pl.BlockSpec(shape, lambda i: (0,) * len(shape))


def anywhere(arrays):
    return [pl.BlockSpec(memory_space=pl.ANY) for _ in arrays]


def params(mib):
    return pltpu.CompilerParams(vmem_limit_bytes=mib * MIB)


def cost(rows, columns, depth):
    return pl.CostEstimate(
        flops=2 * rows * columns * depth, bytes_accessed=2 * depth * (rows + columns), transcendentals=0
    )


def by_strips(step, operands, outs, after=(), passed=()):
    width = operands[0][0].shape[1]
    block = 2 * BLOCK

    def kernel(*refs):
        taken = refs[: len(operands)]
        given = refs[len(operands) + len(after) + len(passed) :]
        for ref, value in zip(given, step(*[ref[...] for ref in taken])):
            ref[...] = value.astype(ref.dtype)

    def strip(rows, at=0):
        return pl.BlockSpec((rows, block), lambda i: (at, i))

    size = sum(rows for _, _, rows in operands) + sum(rows for rows, _ in outs)
    return pl.pallas_call(
        kernel,
        grid=(width // block,),
        in_specs=[strip(rows, start // rows) for _, start, rows in operands]
        + anywhere(after)
        + anywhere(passed),
        out_specs=[strip(rows) for rows, _ in outs] + anywhere(passed),
        out_shape=[jax.ShapeDtypeStruct((rows, width), dtype) for rows, dtype in outs]
        + [jax.ShapeDtypeStruct(array.shape, array.dtype) for array in passed],
        input_output_aliases={len(operands) + len(after) + i: len(outs) + i for i in range(len(passed))},
        compiler_params=params(28),
        cost_estimate=pl.CostEstimate(flops=0, bytes_accessed=2 * size * width, transcendentals=0),
    )(*[array for array, _, _ in operands], *after, *passed)


def all_rows(*arrays):
    return [(array, 0, array.shape[0]) for array in arrays]


def norm_kernel(core_ref, hidden_ref, gain_ref, digits_ref, own_ref):
    width = hidden_ref.shape[1]
    hfloat = wide(hidden_ref[...])
    scale = lax.rsqrt(jnp.mean(hfloat * hfloat, axis=-1, keepdims=True) + 1e-06)
    own_ref[:, :width] = short(hfloat * scale * gain_ref[...])
    own_ref[:, width:] = digits_ref[...]


def normed_half(hidden, gain, digits, core):
    rows, width = hidden.shape
    block = rows // 4
    return pl.pallas_call(
        norm_kernel,
        grid_spec=pltpu.PrefetchScalarGridSpec(
            num_scalar_prefetch=1,
            grid=(2,),
            in_specs=[
                pl.BlockSpec((block, width), lambda i, core_ref: (core_ref[0] * 2 + i, 0)),
                pl.BlockSpec((1, width), lambda i, core_ref: (0, 0)),
                pl.BlockSpec((block, LANES), lambda i, core_ref: (core_ref[0] * 2 + i, 0)),
            ],
            out_specs=pl.BlockSpec((block, width + LANES), lambda i, core_ref: (i, 0)),
        ),
        out_shape=jax.ShapeDtypeStruct((rows // 2, width + LANES), half),
        compiler_params=params(28),
        cost_estimate=pl.CostEstimate(flops=0, bytes_accessed=16 * rows * width, transcendentals=0),
    )(core.reshape(1), hidden, gain.reshape(1, width), digits)


def stack_of(refs):
    return jnp.concatenate([ref[...] for ref in refs], axis=0)


def logits_kernel(n_head, n_token, *refs):
    head = stack_of(refs[:n_head])
    tokens = stack_of(refs[n_head : n_head + n_token])
    digit_refs = refs[n_head + n_token : n_head + 2 * n_token]
    logits_ref, stats_ref = refs[-2:]
    product = lax.dot_general(head, tokens, (((1,), (1,)), ((), ())), preferred_element_type=jnp.float32)
    step = pl.program_id(0)

    @pl.when(step == 0)
    def _():
        logits_ref[...] = product

    @pl.when(step > 0)
    def _():
        logits_ref[...] += product

    @pl.when(step == pl.num_programs(0) - 1)
    def _():
        logits = logits_ref[...]
        top = jnp.max(logits, axis=0, keepdims=True)
        stats_ref[0:1, :] = top
        stats_ref[1:2, :] = jnp.sum(jnp.exp(logits - top), axis=0, keepdims=True)
        digits = wide(stack_of(digit_refs)).T
        stats_ref[2:3, :] = digits[0:1, :] * float(LANES) + digits[1:2, :]


def all_logits(head, tokens, after=()):
    rows, columns = (sum(piece.shape[0] for piece in pieces) for pieces in (head, tokens))
    width = head[0].shape[1]
    digits = [pl.BlockSpec((piece.shape[0], LANES), lambda i: (0, width // LANES)) for piece in tokens]
    return pl.pallas_call(
        lambda *refs: logits_kernel(len(head), len(tokens), *refs),
        grid=(width // BLOCK,),
        in_specs=strips(head) + strips(tokens) + digits + anywhere(after),
        out_specs=[whole((rows, columns)), whole((3, columns))],
        out_shape=[
            jax.ShapeDtypeStruct((rows, columns), jnp.float32),
            jax.ShapeDtypeStruct((3, columns), jnp.float32),
        ],
        compiler_params=params(28),
        cost_estimate=cost(rows, columns, width),
    )(*head, *tokens, *tokens, *after)


def spread(product, outs, part):
    for k, ref in enumerate(outs):
        ref[...] = product[k * part : (k + 1) * part]


def token_grad_kernel(n_head, part, near_ref, flip_ref, stats_ref, wanted_ref, *refs):
    grads_ref = refs[n_head]
    outs, turned_ref = refs[n_head + 1 : -1], refs[-1]

    @pl.when(pl.program_id(0) == 0)
    def _():
        logits = jnp.concatenate([near_ref[...], flip_ref[...]], axis=1)
        rows = lax.broadcasted_iota(jnp.int32, logits.shape, 0)
        share = jnp.exp(logits - stats_ref[0:1, :]) / stats_ref[1:2, :]
        grads = share - jnp.where(rows == wanted_ref[...], 1.0, 0.0)
        grads_ref[...] = short(grads)
        turned_ref[...] = short(grads.T)

    product = jnp.dot(turned_ref[...], stack_of(refs[:n_head]), preferred_element_type=jnp.float32)
    spread(short(product), outs, part)


def token_grads(near, flip, stats, wanted, head):
    rows, columns = near.shape[0], near.shape[1] + flip.shape[1]
    width, part = head[0].shape[1], columns // 8
    return pl.pallas_call(
        lambda *refs: token_grad_kernel(len(head), part, *refs),
        grid=(width // BLOCK,),
        in_specs=[whole(near.shape), whole(flip.shape), whole((2, columns)), whole((1, columns))] + strips(head),
        out_specs=[whole((rows, columns))] + [pl.BlockSpec((part, BLOCK), lambda i: (0, i))] * 8,
        out_shape=[jax.ShapeDtypeStruct((rows, columns), half)] + [jax.ShapeDtypeStruct((part, width), half)] * 8,
        scratch_shapes=[pltpu.VMEM((columns, rows), half)],
        compiler_params=params(56),
        cost_estimate=cost(rows, columns, width),
    )(near, flip, stats, wanted, *head)


def head_grad_kernel(n_head, n_token, grads_ref, *refs):
    near_ref, other_ref, gain_ref = refs[n_head + n_token :]
    tokens = stack_of(refs[n_head : n_head + n_token])
    product = jnp.dot(grads_ref[...], tokens, preferred_element_type=jnp.float32)
    rows = near_ref.shape[0]
    near_ref[...] = product[:rows]
    other_ref[...] = short(product[rows:])
    gain_ref[...] = jnp.sum(product * wide(stack_of(refs[:n_head])), axis=0, keepdims=True)


def head_grads(grads, head, tokens):
    rows, columns = grads.shape
    width = head[0].shape[1]
    return pl.pallas_call(
        lambda *refs: head_grad_kernel(len(head), len(tokens), *refs),
        grid=(width // BLOCK,),
        in_specs=[whole((rows, columns))] + strips(head) + strips(tokens),
        out_specs=[pl.BlockSpec((size, BLOCK), lambda i: (0, i)) for size in (rows // 2, rows // 2, 1)],
        out_shape=[
            jax.ShapeDtypeStruct((rows // 2, width), jnp.float32),
            jax.ShapeDtypeStruct((rows // 2, width), half),
            jax.ShapeDtypeStruct((1, width), jnp.float32),
        ],
        compiler_params=params(28),
        cost_estimate=cost(rows, columns, width),
    )(grads, *head, *tokens)


def hidden_grad_kernel(core_ref, mine_ref, their_ref, hidden_ref, gain_ref, *refs):
    hfloat = wide(hidden_ref[...])
    scale = lax.rsqrt(jnp.mean(hfloat * hfloat, axis=-1, keepdims=True) + 1e-06)
    scaled = (wide(mine_ref[...]) + wide(their_ref[...])) * gain_ref[...]
    dot_mean = jnp.mean(scaled * hfloat, axis=-1, keepdims=True)
    grads = short(scale * scaled - hfloat * scale**3 * dot_mean)
    for ref in refs[-2:]:
        ref[...] = grads


def hidden_grads(mine, their, hidden, gain, core, after):
    rows, width = hidden.shape
    block = rows // 4
    return pl.pallas_call(
        hidden_grad_kernel,
        grid_spec=pltpu.PrefetchScalarGridSpec(
            num_scalar_prefetch=1,
            grid=(2,),
            in_specs=[
                pl.BlockSpec((block, width), lambda i, core_ref: (i, 0)),
                pl.BlockSpec((block, width), lambda i, core_ref: (i, 0)),
                pl.BlockSpec((block, width), lambda i, core_ref: (core_ref[0] * 2 + i, 0)),
                pl.BlockSpec((1, width), lambda i, core_ref: (0, 0)),
            ]
            + anywhere(after),
            out_specs=[
                pl.BlockSpec((block, width), lambda i, core_ref: (i, 0)),
                pl.BlockSpec((block, width), lambda i, core_ref: (core_ref[0] * 2 + i, 0)),
            ],
        ),
        out_shape=[jax.ShapeDtypeStruct((size, width), half) for size in (rows // 2, rows)],
        compiler_params=params(28),
        cost_estimate=pl.CostEstimate(flops=0, bytes_accessed=4 * rows * width, transcendentals=0),
    )(core.reshape(1), mine, their, hidden, gain.reshape(1, width), *after)


def local(hidden, gain, head_weight, first_moment, second_moment, targets):
    core = lax.axis_index("core")
    rows, width = hidden.shape
    held = head_weight.shape[0]
    part = rows // 2

    lane = lax.broadcasted_iota(jnp.int32, (rows, LANES), 1)
    wanted = targets[:, None]
    digits = jnp.where(lane == 0, wanted // LANES, jnp.where(lane == 1, wanted % LANES, 0)).astype(half)
    head_after, head_before = along_z(head_weight, -1), along_z(head_weight, 1)
    own = normed_half(hidden, gain, digits, core)
    own_after, own_before = along_y(own, -1), along_y(own, 1)
    flip_own = flip_x(own)
    own_after, own_before, flip_own = together(own_after, own_before, flip_own)
    own_far = along_y(own_after, -1)
    flip_after = flip_x(own_after)
    head_far = along_z(head_after, -1)
    other_own, other_after, other_before = (along_core(block) for block in (head_weight, head_after, head_before))
    own_far, flip_after = together(own_far, flip_after)
    flip_before = along_y(flip_own, 1)
    flip_far = flip_x(own_far)
    other_far = along_core(head_far)

    head = [head_weight, head_after, head_far, head_before, other_own, other_after, other_far, other_before]
    near_tokens = [own, own_after, own_far, own_before, flip_own, flip_after]
    flip_tokens = [flip_far, flip_before]
    near_logits, near_stats = all_logits(head, near_tokens)
    flip_logits, flip_stats = all_logits(head, flip_tokens, after=[near_stats])

    stats = jnp.concatenate([near_stats[:2], flip_stats[:2]], axis=1).reshape(2, 2, 4, part)
    stats = merge(jnp.stack([stats] + [jnp.roll(along_y(stats, by), -by, axis=2) for by in (1, 2, 3)]))
    stats = merge(jnp.stack([stats] + [jnp.roll(along_x(stats, by), by, axis=1) for by in (1, 2, 3)]))
    stats = stats.reshape(2, 8 * part)
    wanted = jnp.concatenate([near_stats[2:], flip_stats[2:]], axis=1).astype(jnp.int32)
    z, others = lax.axis_index("z"), lax.axis_index("xl") * 16 + lax.axis_index("y")
    spot = jnp.full_like(wanted, -1)
    for other in range(2):
        at_core = (core + other) % 2
        block = lax.axis_index("xh") * 2 + at_core
        for step in range(4):
            start = (block * 32 + others + (z + step * (1 - 2 * at_core)) % 4 * 4) * held
            inside = (wanted >= start) & (wanted < start + held)
            spot = jnp.where(inside, wanted - start + (other * 4 + step) * held, spot)

    grads, sum_own, sum_after, sum_far, sum_before, flip_own, flip_after, flip_far, flip_before = token_grads(
        near_logits, flip_logits, stats, spot, head
    )
    flip_far = flip_x(flip_far)
    flip_before = along_y(flip_before, -1)
    near_head, other_head, gain_sum = head_grads(grads, head, near_tokens + flip_tokens)

    sum_far, gain_sum, other_head, flip_after, sum_before = by_strips(
        lambda far, f_far, g_sum: (wide(far) + wide(f_far), g_sum),
        all_rows(sum_far, flip_far, gain_sum),
        [(part, half), (1, jnp.float32)],
        after=[flip_before],
        passed=[other_head, flip_after, sum_before],
    )
    sum_far = along_y(sum_far, 1)
    flip_after = flip_x(flip_after)
    other_head = along_core(other_head)
    sum_before = along_y(sum_before, -1)
    gain_sum = gain_sum + move(gain_sum, lambda x, core, z, y: (x, core, z ^ 1, y))
    gain_sum = gain_sum + move(gain_sum, lambda x, core, z, y: (x, core, z + 2, y))
    gain_other = along_core(gain_sum)
    head_far, head_before, gain_sum = by_strips(
        lambda mine, theirs, mine_too, theirs_too, g_sum, g_other: (
            mine + wide(theirs),
            mine_too + wide(theirs_too),
            g_sum + g_other,
        ),
        [(near_head, 2 * held, held), (other_head, 2 * held, held)]
        + [(near_head, 3 * held, held), (other_head, 3 * held, held)]
        + all_rows(gain_sum, gain_other),
        [(held, half), (held, half), (1, jnp.float32)],
    )
    head_far = along_z(head_far, 1)

    sum_after, flip_own, gain_sum = by_strips(
        lambda after, f_after, far, own, before: (wide(after) + wide(f_after) + wide(far), wide(own) + wide(before)),
        all_rows(sum_after, flip_after, sum_far, flip_own, flip_before),
        [(part, half), (part, half)],
        after=[sum_before],
        passed=[gain_sum],
    )
    sum_after = along_y(sum_after, 1)
    flip_own = flip_x(flip_own)
    gain_other = move(gain_sum, lambda x, core, z, y: (x ^ 1, core, z, y))

    head_after, gain_sum, head_before = by_strips(
        lambda mine, theirs, far, g_sum, g_other: (mine + wide(theirs) + wide(far), g_sum + g_other),
        [(near_head, held, held), (other_head, held, held)] + all_rows(head_far, gain_sum, gain_other),
        [(held, half), (1, jnp.float32)],
        after=[sum_after],
        passed=[head_before],
    )

    (summed,) = by_strips(
        lambda a, b, c, d: (wide(a) + wide(b) + (wide(c) + wide(d)),),
        all_rows(sum_own, flip_own, sum_after, sum_before),
        [(part, half)],
        after=[head_after],
    )
    head_after, head_before = along_z(head_after, 1), along_z(head_before, -1)
    grad_hidden, placed = hidden_grads(summed, along_x(summed, 2), hidden, gain, core, [])
    other_half = along_core(grad_hidden)
    grad_hidden = lax.dynamic_update_slice(placed, other_half, ((1 - core) * part, 0))

    gain_sum = gain_sum + move(gain_sum, lambda x, core, z, y: (x, core, z, y ^ 1))
    gain_sum = gain_sum + move(gain_sum, lambda x, core, z, y: (x, core, z, y + 2))
    grad_gain = gain_sum + along_x(gain_sum, 2)
    grad_gain = grad_gain.reshape(width) / gain

    grad_head = near_head[:held] + wide(other_head[:held]) + wide(head_after) + wide(head_before)
    new_weight, new_first, new_second = adam_step(head_weight, first_moment, second_moment, grad_head)
    return (grad_hidden, grad_gain, new_weight, new_first, new_second)


def solution(mesh):
    fine = Mesh(mesh.devices.reshape(SIZES), AXES)
    dp = ("xl", "z", "y")
    rows = P(AXES, None)
    return jax.shard_map(
        local,
        mesh=fine,
        in_specs=(P(dp, None), P(), rows, rows, rows, P(dp)),
        out_specs=(P(dp, None), P(), rows, rows, rows),
        check_vma=False,
    )
```

```python
import jax
import jax.numpy as jnp
from jax import lax
from jax.experimental import pallas as pl
from jax.experimental.pallas import tpu as pltpu
from jax.sharding import Mesh
from jax.sharding import PartitionSpec as P

STEP = 100
AXES = ("xh", "core", "xl", "z", "y")
SIZES = (2, 2, 2, 4, 4)
MIB = 1024 * 1024
BLOCK = 1792
LANES = 128
half = jnp.bfloat16


def adam_step(weight, first, second, grads):
    new_first = 0.9 * first + 0.1 * grads
    new_second = 0.95 * second + 0.05 * grads * grads
    corr_one = 1.0 - 0.9**STEP
    corr_two = 1.0 - 0.95**STEP
    wfloat = weight.astype(jnp.float32)
    update = new_first / corr_one / (jnp.sqrt(new_second / corr_two) + 1e-08) + 0.1 * wfloat
    return ((wfloat - 0.001 * update).astype(jnp.bfloat16), new_first, new_second)


def place(x, core, z, y):
    index = 0
    for size, at in zip(SIZES, (x // 2, core, x % 2, z, y)):
        index = index * size + at
    return index


def move(array, step):
    pairs = []
    for x in range(4):
        for core in range(2):
            for z in range(4):
                for y in range(4):
                    x_to, core_to, z_to, y_to = step(x, core, z, y)
                    pairs.append((place(x, core, z, y), place(x_to % 4, core_to % 2, z_to % 4, y_to % 4)))
    return lax.ppermute(array, AXES, pairs)


def along_core(array):
    return move(array, lambda x, core, z, y: (x, core + 1, z, y))


def along_x(array, by):
    return move(array, lambda x, core, z, y: (x + by, core, z, y))


def flip_x(array):
    return move(array, lambda x, core, z, y: (x + 1 - 2 * core, core, z, y))


def along_y(array, by):
    return move(array, lambda x, core, z, y: (x, core, z, y + by * (1 - 2 * core)))


def along_z(array, by):
    return move(array, lambda x, core, z, y: (x, core, z + by * (1 - 2 * core), y))


def short(array):
    return array.astype(jnp.bfloat16)


def wide(array):
    return array.astype(jnp.float32)


def together(*arrays):
    return lax.optimization_barrier(arrays)


def merge(stats):
    top = jnp.max(stats[:, 0], axis=0)
    total = jnp.sum(stats[:, 1] * jnp.exp(stats[:, 0] - top), axis=0)
    return jnp.stack([top, total])


def strips(pieces):
    return [pl.BlockSpec((piece.shape[0], BLOCK), lambda i: (0, i)) for piece in pieces]


def whole(shape):
    return pl.BlockSpec(shape, lambda i: (0,) * len(shape))


def anywhere(arrays):
    return [pl.BlockSpec(memory_space=pl.ANY) for _ in arrays]


def params(mib):
    return pltpu.CompilerParams(vmem_limit_bytes=mib * MIB)


def cost(rows, columns, depth):
    return pl.CostEstimate(
        flops=2 * rows * columns * depth, bytes_accessed=2 * depth * (rows + columns), transcendentals=0
    )


def by_strips(step, operands, outs, after=(), passed=()):
    width = operands[0][0].shape[1]
    block = 2 * BLOCK

    def kernel(*refs):
        taken = refs[: len(operands)]
        given = refs[len(operands) + len(after) + len(passed) :]
        for ref, value in zip(given, step(*[ref[...] for ref in taken])):
            ref[...] = value.astype(ref.dtype)

    def strip(rows, at=0):
        return pl.BlockSpec((rows, block), lambda i: (at, i))

    size = sum(rows for _, _, rows in operands) + sum(rows for rows, _ in outs)
    return pl.pallas_call(
        kernel,
        grid=(width // block,),
        in_specs=[strip(rows, start // rows) for _, start, rows in operands]
        + anywhere(after)
        + anywhere(passed),
        out_specs=[strip(rows) for rows, _ in outs] + anywhere(passed),
        out_shape=[jax.ShapeDtypeStruct((rows, width), dtype) for rows, dtype in outs]
        + [jax.ShapeDtypeStruct(array.shape, array.dtype) for array in passed],
        input_output_aliases={len(operands) + len(after) + i: len(outs) + i for i in range(len(passed))},
        compiler_params=params(28),
        cost_estimate=pl.CostEstimate(flops=0, bytes_accessed=2 * size * width, transcendentals=0),
    )(*[array for array, _, _ in operands], *after, *passed)


def all_rows(*arrays):
    return [(array, 0, array.shape[0]) for array in arrays]


def norm_kernel(core_ref, hidden_ref, gain_ref, digits_ref, own_ref):
    width = hidden_ref.shape[1]
    hfloat = wide(hidden_ref[...])
    scale = lax.rsqrt(jnp.mean(hfloat * hfloat, axis=-1, keepdims=True) + 1e-06)
    own_ref[:, :width] = short(hfloat * scale * gain_ref[...])
    own_ref[:, width:] = digits_ref[...]


def normed_half(hidden, gain, digits, core):
    rows, width = hidden.shape
    block = rows // 4
    return pl.pallas_call(
        norm_kernel,
        grid_spec=pltpu.PrefetchScalarGridSpec(
            num_scalar_prefetch=1,
            grid=(2,),
            in_specs=[
                pl.BlockSpec((block, width), lambda i, core_ref: (core_ref[0] * 2 + i, 0)),
                pl.BlockSpec((1, width), lambda i, core_ref: (0, 0)),
                pl.BlockSpec((block, LANES), lambda i, core_ref: (core_ref[0] * 2 + i, 0)),
            ],
            out_specs=pl.BlockSpec((block, width + LANES), lambda i, core_ref: (i, 0)),
        ),
        out_shape=jax.ShapeDtypeStruct((rows // 2, width + LANES), half),
        compiler_params=params(28),
        cost_estimate=pl.CostEstimate(flops=0, bytes_accessed=16 * rows * width, transcendentals=0),
    )(core.reshape(1), hidden, gain.reshape(1, width), digits)


def stack_of(refs):
    return jnp.concatenate([ref[...] for ref in refs], axis=0)


def logits_kernel(n_head, n_token, *refs):
    head = stack_of(refs[:n_head])
    tokens = stack_of(refs[n_head : n_head + n_token])
    digit_refs = refs[n_head + n_token : n_head + 2 * n_token]
    logits_ref, stats_ref = refs[-2:]
    product = lax.dot_general(head, tokens, (((1,), (1,)), ((), ())), preferred_element_type=jnp.float32)
    step = pl.program_id(0)

    @pl.when(step == 0)
    def _():
        logits_ref[...] = product

    @pl.when(step > 0)
    def _():
        logits_ref[...] += product

    @pl.when(step == pl.num_programs(0) - 1)
    def _():
        logits = logits_ref[...]
        top = jnp.max(logits, axis=0, keepdims=True)
        stats_ref[0:1, :] = top
        stats_ref[1:2, :] = jnp.sum(jnp.exp(logits - top), axis=0, keepdims=True)
        digits = wide(stack_of(digit_refs)).T
        stats_ref[2:3, :] = digits[0:1, :] * float(LANES) + digits[1:2, :]


def all_logits(head, tokens, after=()):
    rows, columns = (sum(piece.shape[0] for piece in pieces) for pieces in (head, tokens))
    width = head[0].shape[1]
    digits = [pl.BlockSpec((piece.shape[0], LANES), lambda i: (0, width // LANES)) for piece in tokens]
    return pl.pallas_call(
        lambda *refs: logits_kernel(len(head), len(tokens), *refs),
        grid=(width // BLOCK,),
        in_specs=strips(head) + strips(tokens) + digits + anywhere(after),
        out_specs=[whole((rows, columns)), whole((3, columns))],
        out_shape=[
            jax.ShapeDtypeStruct((rows, columns), jnp.float32),
            jax.ShapeDtypeStruct((3, columns), jnp.float32),
        ],
        compiler_params=params(28),
        cost_estimate=cost(rows, columns, width),
    )(*head, *tokens, *tokens, *after)


def spread(product, outs, part):
    for k, ref in enumerate(outs):
        ref[...] = product[k * part : (k + 1) * part]


def token_grad_kernel(n_head, part, near_ref, flip_ref, stats_ref, wanted_ref, *refs):
    grads_ref = refs[n_head]
    outs, turned_ref = refs[n_head + 1 : -1], refs[-1]

    @pl.when(pl.program_id(0) == 0)
    def _():
        logits = jnp.concatenate([near_ref[...], flip_ref[...]], axis=1)
        rows = lax.broadcasted_iota(jnp.int32, logits.shape, 0)
        share = jnp.exp(logits - stats_ref[0:1, :]) / stats_ref[1:2, :]
        grads = share - jnp.where(rows == wanted_ref[...], 1.0, 0.0)
        grads_ref[...] = short(grads)
        turned_ref[...] = short(grads.T)

    product = jnp.dot(turned_ref[...], stack_of(refs[:n_head]), preferred_element_type=jnp.float32)
    spread(short(product), outs, part)


def token_grads(near, flip, stats, wanted, head):
    rows, columns = near.shape[0], near.shape[1] + flip.shape[1]
    width, part = head[0].shape[1], columns // 8
    return pl.pallas_call(
        lambda *refs: token_grad_kernel(len(head), part, *refs),
        grid=(width // BLOCK,),
        in_specs=[whole(near.shape), whole(flip.shape), whole((2, columns)), whole((1, columns))] + strips(head),
        out_specs=[whole((rows, columns))] + [pl.BlockSpec((part, BLOCK), lambda i: (0, i))] * 8,
        out_shape=[jax.ShapeDtypeStruct((rows, columns), half)] + [jax.ShapeDtypeStruct((part, width), half)] * 8,
        scratch_shapes=[pltpu.VMEM((columns, rows), half)],
        compiler_params=params(56),
        cost_estimate=cost(rows, columns, width),
    )(near, flip, stats, wanted, *head)


def head_grad_kernel(n_head, n_token, grads_ref, *refs):
    near_ref, other_ref, gain_ref = refs[n_head + n_token :]
    tokens = stack_of(refs[n_head : n_head + n_token])
    product = jnp.dot(grads_ref[...], tokens, preferred_element_type=jnp.float32)
    rows = near_ref.shape[0]
    near_ref[...] = product[:rows]
    other_ref[...] = short(product[rows:])
    gain_ref[...] = jnp.sum(product * wide(stack_of(refs[:n_head])), axis=0, keepdims=True)


def head_grads(grads, head, tokens):
    rows, columns = grads.shape
    width = head[0].shape[1]
    return pl.pallas_call(
        lambda *refs: head_grad_kernel(len(head), len(tokens), *refs),
        grid=(width // BLOCK,),
        in_specs=[whole((rows, columns))] + strips(head) + strips(tokens),
        out_specs=[pl.BlockSpec((size, BLOCK), lambda i: (0, i)) for size in (rows // 2, rows // 2, 1)],
        out_shape=[
            jax.ShapeDtypeStruct((rows // 2, width), jnp.float32),
            jax.ShapeDtypeStruct((rows // 2, width), half),
            jax.ShapeDtypeStruct((1, width), jnp.float32),
        ],
        compiler_params=params(28),
        cost_estimate=cost(rows, columns, width),
    )(grads, *head, *tokens)


def hidden_grad_kernel(core_ref, mine_ref, their_ref, hidden_ref, gain_ref, *refs):
    hfloat = wide(hidden_ref[...])
    scale = lax.rsqrt(jnp.mean(hfloat * hfloat, axis=-1, keepdims=True) + 1e-06)
    scaled = (wide(mine_ref[...]) + wide(their_ref[...])) * gain_ref[...]
    dot_mean = jnp.mean(scaled * hfloat, axis=-1, keepdims=True)
    grads = short(scale * scaled - hfloat * scale**3 * dot_mean)
    for ref in refs[-2:]:
        ref[...] = grads


def hidden_grads(mine, their, hidden, gain, core, after):
    rows, width = hidden.shape
    block = rows // 4
    return pl.pallas_call(
        hidden_grad_kernel,
        grid_spec=pltpu.PrefetchScalarGridSpec(
            num_scalar_prefetch=1,
            grid=(2,),
            in_specs=[
                pl.BlockSpec((block, width), lambda i, core_ref: (i, 0)),
                pl.BlockSpec((block, width), lambda i, core_ref: (i, 0)),
                pl.BlockSpec((block, width), lambda i, core_ref: (core_ref[0] * 2 + i, 0)),
                pl.BlockSpec((1, width), lambda i, core_ref: (0, 0)),
            ]
            + anywhere(after),
            out_specs=[
                pl.BlockSpec((block, width), lambda i, core_ref: (i, 0)),
                pl.BlockSpec((block, width), lambda i, core_ref: (core_ref[0] * 2 + i, 0)),
            ],
        ),
        out_shape=[jax.ShapeDtypeStruct((size, width), half) for size in (rows // 2, rows)],
        compiler_params=params(28),
        cost_estimate=pl.CostEstimate(flops=0, bytes_accessed=4 * rows * width, transcendentals=0),
    )(core.reshape(1), mine, their, hidden, gain.reshape(1, width), *after)


def local(hidden, gain, head_weight, first_moment, second_moment, targets):
    core = lax.axis_index("core")
    rows, width = hidden.shape
    held = head_weight.shape[0]
    part = rows // 2

    lane = lax.broadcasted_iota(jnp.int32, (rows, LANES), 1)
    wanted = targets[:, None]
    digits = jnp.where(lane == 0, wanted // LANES, jnp.where(lane == 1, wanted % LANES, 0)).astype(half)
    head_after, head_before = along_z(head_weight, -1), along_z(head_weight, 1)
    own = normed_half(hidden, gain, digits, core)
    own_after, own_before = along_y(own, -1), along_y(own, 1)
    flip_own = flip_x(own)
    own_after, own_before, flip_own = together(own_after, own_before, flip_own)
    own_far = along_y(own_after, -1)
    flip_after = flip_x(own_after)
    head_far = along_z(head_after, -1)
    other_own, other_after, other_before = (along_core(block) for block in (head_weight, head_after, head_before))
    own_far, flip_after = together(own_far, flip_after)
    flip_before = along_y(flip_own, 1)
    flip_far = flip_x(own_far)
    other_far = along_core(head_far)

    head = [head_weight, head_after, head_far, head_before, other_own, other_after, other_far, other_before]
    near_tokens = [own, own_after, own_far, own_before, flip_own, flip_after]
    flip_tokens = [flip_far, flip_before]
    near_logits, near_stats = all_logits(head, near_tokens)
    flip_logits, flip_stats = all_logits(head, flip_tokens, after=[near_stats])

    stats = jnp.concatenate([near_stats[:2], flip_stats[:2]], axis=1).reshape(2, 2, 4, part)
    stats = merge(jnp.stack([stats] + [jnp.roll(along_y(stats, by), -by, axis=2) for by in (1, 2, 3)]))
    stats = merge(jnp.stack([stats] + [jnp.roll(along_x(stats, by), by, axis=1) for by in (1, 2, 3)]))
    stats = stats.reshape(2, 8 * part)
    wanted = jnp.concatenate([near_stats[2:], flip_stats[2:]], axis=1).astype(jnp.int32)
    z, others = lax.axis_index("z"), lax.axis_index("xl") * 16 + lax.axis_index("y")
    spot = jnp.full_like(wanted, -1)
    for other in range(2):
        at_core = (core + other) % 2
        block = lax.axis_index("xh") * 2 + at_core
        for step in range(4):
            start = (block * 32 + others + (z + step * (1 - 2 * at_core)) % 4 * 4) * held
            inside = (wanted >= start) & (wanted < start + held)
            spot = jnp.where(inside, wanted - start + (other * 4 + step) * held, spot)

    grads, sum_own, sum_after, sum_far, sum_before, flip_own, flip_after, flip_far, flip_before = token_grads(
        near_logits, flip_logits, stats, spot, head
    )
    flip_far = flip_x(flip_far)
    flip_before = along_y(flip_before, -1)
    near_head, other_head, gain_sum = head_grads(grads, head, near_tokens + flip_tokens)

    sum_far, gain_sum, other_head, flip_after, sum_before = by_strips(
        lambda far, f_far, g_sum: (wide(far) + wide(f_far), g_sum),
        all_rows(sum_far, flip_far, gain_sum),
        [(part, half), (1, jnp.float32)],
        after=[flip_before],
        passed=[other_head, flip_after, sum_before],
    )
    sum_far = along_y(sum_far, 1)
    flip_after = flip_x(flip_after)
    other_head = along_core(other_head)
    sum_before = along_y(sum_before, -1)
    gain_sum = gain_sum + move(gain_sum, lambda x, core, z, y: (x, core, z ^ 1, y))
    gain_sum = gain_sum + move(gain_sum, lambda x, core, z, y: (x, core, z + 2, y))
    gain_other = along_core(gain_sum)
    head_far, head_before, gain_sum = by_strips(
        lambda mine, theirs, mine_too, theirs_too, g_sum, g_other: (
            mine + wide(theirs),
            mine_too + wide(theirs_too),
            g_sum + g_other,
        ),
        [(near_head, 2 * held, held), (other_head, 2 * held, held)]
        + [(near_head, 3 * held, held), (other_head, 3 * held, held)]
        + all_rows(gain_sum, gain_other),
        [(held, half), (held, half), (1, jnp.float32)],
    )
    head_far = along_z(head_far, 1)

    sum_after, flip_own, head_before, gain_sum = by_strips(
        lambda after, f_after, far, own, before: (wide(after) + wide(f_after) + wide(far), wide(own) + wide(before)),
        all_rows(sum_after, flip_after, sum_far, flip_own, flip_before),
        [(part, half), (part, half)],
        after=[sum_before],
        passed=[head_before, gain_sum],
    )
    sum_after = along_y(sum_after, 1)
    flip_own = flip_x(flip_own)
    head_before = along_z(head_before, -1)
    gain_other = move(gain_sum, lambda x, core, z, y: (x ^ 1, core, z, y))

    (gain_sum,) = by_strips(
        lambda mine, theirs: (mine + theirs,), all_rows(gain_sum, gain_other), [(1, jnp.float32)]
    )

    (summed,) = by_strips(
        lambda a, b, c, d: (wide(a) + wide(b) + (wide(c) + wide(d)),),
        all_rows(sum_own, flip_own, sum_after, sum_before),
        [(part, half)],
        after=[gain_sum],
    )
    gain_other = move(gain_sum, lambda x, core, z, y: (x, core, z, y ^ 1))
    (head_after,) = by_strips(
        lambda mine, theirs, far: (mine + wide(theirs) + wide(far),),
        [(near_head, held, held), (other_head, held, held), (head_far, 0, held)],
        [(held, half)],
        after=[summed, gain_other],
    )
    head_after = along_z(head_after, 1)
    grad_hidden, placed = hidden_grads(summed, along_x(summed, 2), hidden, gain, core, [])
    other_half = along_core(grad_hidden)
    grad_hidden = lax.dynamic_update_slice(placed, other_half, ((1 - core) * part, 0))

    gain_sum = gain_sum + gain_other
    gain_sum = gain_sum + move(gain_sum, lambda x, core, z, y: (x, core, z, y + 2))
    grad_gain = gain_sum + along_x(gain_sum, 2)
    grad_gain = grad_gain.reshape(width) / gain

    grad_head = near_head[:held] + wide(other_head[:held]) + wide(head_after) + wide(head_before)
    new_weight, new_first, new_second = adam_step(head_weight, first_moment, second_moment, grad_head)
    return (grad_hidden, grad_gain, new_weight, new_first, new_second)


def solution(mesh):
    fine = Mesh(mesh.devices.reshape(SIZES), AXES)
    dp = ("xl", "z", "y")
    rows = P(AXES, None)
    return jax.shard_map(
        local,
        mesh=fine,
        in_specs=(P(dp, None), P(), rows, rows, rows, P(dp)),
        out_specs=(P(dp, None), P(), rows, rows, rows),
        check_vma=False,
    )
```

```python
import jax
import jax.numpy as jnp
from jax import lax
from jax.experimental import pallas as pl
from jax.experimental.pallas import tpu as pltpu
from jax.sharding import Mesh
from jax.sharding import PartitionSpec as P

STEP = 100
AXES = ("xh", "core", "xl", "z", "y")
SIZES = (2, 2, 2, 4, 4)
MIB = 1024 * 1024
BLOCK = 1792
LANES = 128
half = jnp.bfloat16


def adam_step(weight, first, second, grads):
    new_first = 0.9 * first + 0.1 * grads
    new_second = 0.95 * second + 0.05 * grads * grads
    corr_one = 1.0 - 0.9**STEP
    corr_two = 1.0 - 0.95**STEP
    wfloat = weight.astype(jnp.float32)
    update = new_first / corr_one / (jnp.sqrt(new_second / corr_two) + 1e-08) + 0.1 * wfloat
    return ((wfloat - 0.001 * update).astype(jnp.bfloat16), new_first, new_second)


def place(x, core, z, y):
    index = 0
    for size, at in zip(SIZES, (x // 2, core, x % 2, z, y)):
        index = index * size + at
    return index


def move(array, step):
    pairs = []
    for x in range(4):
        for core in range(2):
            for z in range(4):
                for y in range(4):
                    x_to, core_to, z_to, y_to = step(x, core, z, y)
                    pairs.append((place(x, core, z, y), place(x_to % 4, core_to % 2, z_to % 4, y_to % 4)))
    return lax.ppermute(array, AXES, pairs)


def along_core(array):
    return move(array, lambda x, core, z, y: (x, core + 1, z, y))


def along_x(array, by):
    return move(array, lambda x, core, z, y: (x + by, core, z, y))


def flip_x(array):
    return move(array, lambda x, core, z, y: (x + 1 - 2 * core, core, z, y))


def along_y(array, by):
    return move(array, lambda x, core, z, y: (x, core, z, y + by * (1 - 2 * core)))


def along_z(array, by):
    return move(array, lambda x, core, z, y: (x, core, z + by * (1 - 2 * core), y))


def short(array):
    return array.astype(jnp.bfloat16)


def wide(array):
    return array.astype(jnp.float32)


def together(*arrays):
    return lax.optimization_barrier(arrays)


def merge(stats):
    top = jnp.max(stats[:, 0], axis=0)
    total = jnp.sum(stats[:, 1] * jnp.exp(stats[:, 0] - top), axis=0)
    return jnp.stack([top, total])


def strips(pieces, block=BLOCK):
    return [pl.BlockSpec((piece.shape[0], block), lambda i: (0, i)) for piece in pieces]


def whole(shape):
    return pl.BlockSpec(shape, lambda i: (0,) * len(shape))


def anywhere(arrays):
    return [pl.BlockSpec(memory_space=pl.ANY) for _ in arrays]


def params(mib):
    return pltpu.CompilerParams(vmem_limit_bytes=mib * MIB)


def cost(rows, columns, depth):
    return pl.CostEstimate(
        flops=2 * rows * columns * depth, bytes_accessed=2 * depth * (rows + columns), transcendentals=0
    )


def by_strips(step, operands, outs, after=(), passed=()):
    width = operands[0][0].shape[1]
    block = 2 * BLOCK

    def kernel(*refs):
        taken = refs[: len(operands)]
        given = refs[len(operands) + len(after) + len(passed) :]
        for ref, value in zip(given, step(*[ref[...] for ref in taken])):
            ref[...] = value.astype(ref.dtype)

    def strip(rows, at=0):
        return pl.BlockSpec((rows, block), lambda i: (at, i))

    size = sum(rows for _, _, rows in operands) + sum(rows for rows, _ in outs)
    return pl.pallas_call(
        kernel,
        grid=(width // block,),
        in_specs=[strip(rows, start // rows) for _, start, rows in operands]
        + anywhere(after)
        + anywhere(passed),
        out_specs=[strip(rows) for rows, _ in outs] + anywhere(passed),
        out_shape=[jax.ShapeDtypeStruct((rows, width), dtype) for rows, dtype in outs]
        + [jax.ShapeDtypeStruct(array.shape, array.dtype) for array in passed],
        input_output_aliases={len(operands) + len(after) + i: len(outs) + i for i in range(len(passed))},
        compiler_params=params(28),
        cost_estimate=pl.CostEstimate(flops=0, bytes_accessed=2 * size * width, transcendentals=0),
    )(*[array for array, _, _ in operands], *after, *passed)


def all_rows(*arrays):
    return [(array, 0, array.shape[0]) for array in arrays]


def norm_kernel(core_ref, hidden_ref, gain_ref, digits_ref, own_ref):
    width = hidden_ref.shape[1]
    hfloat = wide(hidden_ref[...])
    scale = lax.rsqrt(jnp.mean(hfloat * hfloat, axis=-1, keepdims=True) + 1e-06)
    own_ref[:, :width] = short(hfloat * scale * gain_ref[...])
    own_ref[:, width:] = digits_ref[...]


def normed_half(hidden, gain, digits, core):
    rows, width = hidden.shape
    block = rows // 4
    return pl.pallas_call(
        norm_kernel,
        grid_spec=pltpu.PrefetchScalarGridSpec(
            num_scalar_prefetch=1,
            grid=(2,),
            in_specs=[
                pl.BlockSpec((block, width), lambda i, core_ref: (core_ref[0] * 2 + i, 0)),
                pl.BlockSpec((1, width), lambda i, core_ref: (0, 0)),
                pl.BlockSpec((block, LANES), lambda i, core_ref: (core_ref[0] * 2 + i, 0)),
            ],
            out_specs=pl.BlockSpec((block, width + LANES), lambda i, core_ref: (i, 0)),
        ),
        out_shape=jax.ShapeDtypeStruct((rows // 2, width + LANES), half),
        compiler_params=params(28),
        cost_estimate=pl.CostEstimate(flops=0, bytes_accessed=16 * rows * width, transcendentals=0),
    )(core.reshape(1), hidden, gain.reshape(1, width), digits)


def stack_of(refs):
    return jnp.concatenate([ref[...] for ref in refs], axis=0)


def logits_kernel(n_head, n_token, *refs):
    head = stack_of(refs[:n_head])
    tokens = stack_of(refs[n_head : n_head + n_token])
    digit_refs = refs[n_head + n_token : n_head + 2 * n_token]
    logits_ref, stats_ref = refs[-2:]
    product = lax.dot_general(head, tokens, (((1,), (1,)), ((), ())), preferred_element_type=jnp.float32)
    step = pl.program_id(0)

    @pl.when(step == 0)
    def _():
        logits_ref[...] = product

    @pl.when(step > 0)
    def _():
        logits_ref[...] += product

    @pl.when(step == pl.num_programs(0) - 1)
    def _():
        logits = logits_ref[...]
        top = jnp.max(logits, axis=0, keepdims=True)
        stats_ref[0:1, :] = top
        stats_ref[1:2, :] = jnp.sum(jnp.exp(logits - top), axis=0, keepdims=True)
        digits = wide(stack_of(digit_refs)).T
        stats_ref[2:3, :] = digits[0:1, :] * float(LANES) + digits[1:2, :]


def all_logits(head, tokens, after=()):
    rows, columns = (sum(piece.shape[0] for piece in pieces) for pieces in (head, tokens))
    width = head[0].shape[1]
    digits = [pl.BlockSpec((piece.shape[0], LANES), lambda i: (0, width // LANES)) for piece in tokens]
    return pl.pallas_call(
        lambda *refs: logits_kernel(len(head), len(tokens), *refs),
        grid=(width // (2 * BLOCK),),
        in_specs=strips(head, 2 * BLOCK) + strips(tokens, 2 * BLOCK) + digits + anywhere(after),
        out_specs=[whole((rows, columns)), whole((3, columns))],
        out_shape=[
            jax.ShapeDtypeStruct((rows, columns), jnp.float32),
            jax.ShapeDtypeStruct((3, columns), jnp.float32),
        ],
        compiler_params=params(28),
        cost_estimate=cost(rows, columns, width),
    )(*head, *tokens, *tokens, *after)


def spread(product, outs, part):
    for k, ref in enumerate(outs):
        ref[...] = product[k * part : (k + 1) * part]


def token_grad_kernel(n_head, part, near_ref, flip_ref, stats_ref, wanted_ref, *refs):
    grads_ref = refs[n_head]
    outs, turned_ref = refs[n_head + 1 : -1], refs[-1]

    @pl.when(pl.program_id(0) == 0)
    def _():
        logits = jnp.concatenate([near_ref[...], flip_ref[...]], axis=1)
        rows = lax.broadcasted_iota(jnp.int32, logits.shape, 0)
        share = jnp.exp(logits - stats_ref[0:1, :]) / stats_ref[1:2, :]
        grads = share - jnp.where(rows == wanted_ref[...], 1.0, 0.0)
        grads_ref[...] = short(grads)
        turned_ref[...] = short(grads.T)

    product = jnp.dot(turned_ref[...], stack_of(refs[:n_head]), preferred_element_type=jnp.float32)
    spread(short(product), outs, part)


def token_grads(near, flip, stats, wanted, head):
    rows, columns = near.shape[0], near.shape[1] + flip.shape[1]
    width, part = head[0].shape[1], columns // 8
    return pl.pallas_call(
        lambda *refs: token_grad_kernel(len(head), part, *refs),
        grid=(width // (2 * BLOCK),),
        in_specs=[whole(near.shape), whole(flip.shape), whole((2, columns)), whole((1, columns))] + strips(head, 2 * BLOCK),
        out_specs=[whole((rows, columns))] + [pl.BlockSpec((part, 2 * BLOCK), lambda i: (0, i))] * 8,
        out_shape=[jax.ShapeDtypeStruct((rows, columns), half)] + [jax.ShapeDtypeStruct((part, width), half)] * 8,
        scratch_shapes=[pltpu.VMEM((columns, rows), half)],
        compiler_params=params(56),
        cost_estimate=cost(rows, columns, width),
    )(near, flip, stats, wanted, *head)


def head_grad_kernel(n_head, n_token, grads_ref, *refs):
    near_ref, other_ref, gain_ref = refs[n_head + n_token :]
    tokens = stack_of(refs[n_head : n_head + n_token])
    product = jnp.dot(grads_ref[...], tokens, preferred_element_type=jnp.float32)
    rows = near_ref.shape[0]
    near_ref[...] = product[:rows]
    other_ref[...] = short(product[rows:])
    gain_ref[...] = jnp.sum(product * wide(stack_of(refs[:n_head])), axis=0, keepdims=True)


def head_grads(grads, head, tokens):
    rows, columns = grads.shape
    width = head[0].shape[1]
    return pl.pallas_call(
        lambda *refs: head_grad_kernel(len(head), len(tokens), *refs),
        grid=(width // BLOCK,),
        in_specs=[whole((rows, columns))] + strips(head) + strips(tokens),
        out_specs=[pl.BlockSpec((size, BLOCK), lambda i: (0, i)) for size in (rows // 2, rows // 2, 1)],
        out_shape=[
            jax.ShapeDtypeStruct((rows // 2, width), jnp.float32),
            jax.ShapeDtypeStruct((rows // 2, width), half),
            jax.ShapeDtypeStruct((1, width), jnp.float32),
        ],
        compiler_params=params(28),
        cost_estimate=cost(rows, columns, width),
    )(grads, *head, *tokens)


def hidden_grad_kernel(core_ref, mine_ref, their_ref, hidden_ref, gain_ref, *refs):
    hfloat = wide(hidden_ref[...])
    scale = lax.rsqrt(jnp.mean(hfloat * hfloat, axis=-1, keepdims=True) + 1e-06)
    scaled = (wide(mine_ref[...]) + wide(their_ref[...])) * gain_ref[...]
    dot_mean = jnp.mean(scaled * hfloat, axis=-1, keepdims=True)
    grads = short(scale * scaled - hfloat * scale**3 * dot_mean)
    for ref in refs[-2:]:
        ref[...] = grads


def hidden_grads(mine, their, hidden, gain, core, after):
    rows, width = hidden.shape
    block = rows // 4
    return pl.pallas_call(
        hidden_grad_kernel,
        grid_spec=pltpu.PrefetchScalarGridSpec(
            num_scalar_prefetch=1,
            grid=(2,),
            in_specs=[
                pl.BlockSpec((block, width), lambda i, core_ref: (i, 0)),
                pl.BlockSpec((block, width), lambda i, core_ref: (i, 0)),
                pl.BlockSpec((block, width), lambda i, core_ref: (core_ref[0] * 2 + i, 0)),
                pl.BlockSpec((1, width), lambda i, core_ref: (0, 0)),
            ]
            + anywhere(after),
            out_specs=[
                pl.BlockSpec((block, width), lambda i, core_ref: (i, 0)),
                pl.BlockSpec((block, width), lambda i, core_ref: (core_ref[0] * 2 + i, 0)),
            ],
        ),
        out_shape=[jax.ShapeDtypeStruct((size, width), half) for size in (rows // 2, rows)],
        compiler_params=params(28),
        cost_estimate=pl.CostEstimate(flops=0, bytes_accessed=4 * rows * width, transcendentals=0),
    )(core.reshape(1), mine, their, hidden, gain.reshape(1, width), *after)


def local(hidden, gain, head_weight, first_moment, second_moment, targets):
    core = lax.axis_index("core")
    rows, width = hidden.shape
    held = head_weight.shape[0]
    part = rows // 2

    lane = lax.broadcasted_iota(jnp.int32, (rows, LANES), 1)
    wanted = targets[:, None]
    digits = jnp.where(lane == 0, wanted // LANES, jnp.where(lane == 1, wanted % LANES, 0)).astype(half)
    head_after, head_before = along_z(head_weight, -1), along_z(head_weight, 1)
    own = normed_half(hidden, gain, digits, core)
    own_after, own_before = along_y(own, -1), along_y(own, 1)
    flip_own = flip_x(own)
    own_after, own_before, flip_own = together(own_after, own_before, flip_own)
    own_far = along_y(own_after, -1)
    flip_after = flip_x(own_after)
    head_far = along_z(head_after, -1)
    other_own, other_after, other_before = (along_core(block) for block in (head_weight, head_after, head_before))
    own_far, flip_after = together(own_far, flip_after)
    flip_before = along_y(flip_own, 1)
    flip_far = flip_x(own_far)
    other_far = along_core(head_far)

    head = [head_weight, head_after, head_far, head_before, other_own, other_after, other_far, other_before]
    near_tokens = [own, own_after, own_far, own_before, flip_own, flip_after]
    flip_tokens = [flip_far, flip_before]
    near_logits, near_stats = all_logits(head, near_tokens)
    flip_logits, flip_stats = all_logits(head, flip_tokens, after=[near_stats])

    stats = jnp.concatenate([near_stats[:2], flip_stats[:2]], axis=1).reshape(2, 2, 4, part)
    stats = merge(jnp.stack([stats] + [jnp.roll(along_y(stats, by), -by, axis=2) for by in (1, 2, 3)]))
    stats = merge(jnp.stack([stats] + [jnp.roll(along_x(stats, by), by, axis=1) for by in (1, 2, 3)]))
    stats = stats.reshape(2, 8 * part)
    wanted = jnp.concatenate([near_stats[2:], flip_stats[2:]], axis=1).astype(jnp.int32)
    z, others = lax.axis_index("z"), lax.axis_index("xl") * 16 + lax.axis_index("y")
    spot = jnp.full_like(wanted, -1)
    for other in range(2):
        at_core = (core + other) % 2
        block = lax.axis_index("xh") * 2 + at_core
        for step in range(4):
            start = (block * 32 + others + (z + step * (1 - 2 * at_core)) % 4 * 4) * held
            inside = (wanted >= start) & (wanted < start + held)
            spot = jnp.where(inside, wanted - start + (other * 4 + step) * held, spot)

    grads, sum_own, sum_after, sum_far, sum_before, flip_own, flip_after, flip_far, flip_before = token_grads(
        near_logits, flip_logits, stats, spot, head
    )
    flip_far = flip_x(flip_far)
    flip_before = along_y(flip_before, -1)
    near_head, other_head, gain_sum = head_grads(grads, head, near_tokens + flip_tokens)

    sum_far, gain_sum, other_head, flip_after, sum_before = by_strips(
        lambda far, f_far, g_sum: (wide(far) + wide(f_far), g_sum),
        all_rows(sum_far, flip_far, gain_sum),
        [(part, half), (1, jnp.float32)],
        after=[flip_before],
        passed=[other_head, flip_after, sum_before],
    )
    sum_far = along_y(sum_far, 1)
    flip_after = flip_x(flip_after)
    other_head = along_core(other_head)
    sum_before = along_y(sum_before, -1)
    gain_sum = gain_sum + move(gain_sum, lambda x, core, z, y: (x, core, z ^ 1, y))
    gain_sum = gain_sum + move(gain_sum, lambda x, core, z, y: (x, core, z + 2, y))
    gain_other = along_core(gain_sum)
    head_far, head_before, gain_sum = by_strips(
        lambda mine, theirs, mine_too, theirs_too, g_sum, g_other: (
            mine + wide(theirs),
            mine_too + wide(theirs_too),
            g_sum + g_other,
        ),
        [(near_head, 2 * held, held), (other_head, 2 * held, held)]
        + [(near_head, 3 * held, held), (other_head, 3 * held, held)]
        + all_rows(gain_sum, gain_other),
        [(held, half), (held, half), (1, jnp.float32)],
    )
    head_far = along_z(head_far, 1)

    sum_after, flip_own, head_before, gain_sum = by_strips(
        lambda after, f_after, far, own, before: (wide(after) + wide(f_after) + wide(far), wide(own) + wide(before)),
        all_rows(sum_after, flip_after, sum_far, flip_own, flip_before),
        [(part, half), (part, half)],
        after=[sum_before],
        passed=[head_before, gain_sum],
    )
    sum_after = along_y(sum_after, 1)
    flip_own = flip_x(flip_own)
    head_before = along_z(head_before, -1)
    gain_other = move(gain_sum, lambda x, core, z, y: (x ^ 1, core, z, y))

    (gain_sum,) = by_strips(
        lambda mine, theirs: (mine + theirs,), all_rows(gain_sum, gain_other), [(1, jnp.float32)]
    )

    (summed,) = by_strips(
        lambda a, b, c, d: (wide(a) + wide(b) + (wide(c) + wide(d)),),
        all_rows(sum_own, flip_own, sum_after, sum_before),
        [(part, half)],
        after=[gain_sum],
    )
    gain_other = move(gain_sum, lambda x, core, z, y: (x, core, z, y ^ 1))
    (head_after,) = by_strips(
        lambda mine, theirs, far: (mine + wide(theirs) + wide(far),),
        [(near_head, held, held), (other_head, held, held), (head_far, 0, held)],
        [(held, half)],
        after=[summed, gain_other],
    )
    head_after = along_z(head_after, 1)
    grad_hidden, placed = hidden_grads(summed, along_x(summed, 2), hidden, gain, core, [])
    other_half = along_core(grad_hidden)
    grad_hidden = lax.dynamic_update_slice(placed, other_half, ((1 - core) * part, 0))

    gain_sum = gain_sum + gain_other
    gain_sum = gain_sum + move(gain_sum, lambda x, core, z, y: (x, core, z, y + 2))
    grad_gain = gain_sum + along_x(gain_sum, 2)
    grad_gain = grad_gain.reshape(width) / gain

    grad_head = near_head[:held] + wide(other_head[:held]) + wide(head_after) + wide(head_before)
    new_weight, new_first, new_second = adam_step(head_weight, first_moment, second_moment, grad_head)
    return (grad_hidden, grad_gain, new_weight, new_first, new_second)


def solution(mesh):
    fine = Mesh(mesh.devices.reshape(SIZES), AXES)
    dp = ("xl", "z", "y")
    rows = P(AXES, None)
    return jax.shard_map(
        local,
        mesh=fine,
        in_specs=(P(dp, None), P(), rows, rows, rows, P(dp)),
        out_specs=(P(dp, None), P(), rows, rows, rows),
        check_vma=False,
    )
```
